32 devices in a mesh: occ: 4 (over y, x), vir: 8 (over z, core).
Axes of the slice: x: 2, y: 2, z: 4, core: 2. Of those that a mesh axis runs over, the one named last changes fastest.
Arguments:
- amplitudes: bfloat16 [64, 8, 64, 4096], P(None, 'vir', 'occ'), may hold values from -6 to 6
- integrals: bfloat16 [64, 32, 64, 4096], P(None, None, 'occ', 'vir'), may hold values from -0.01171875 to 0.01171875
- screen: int32 [8, 64, 64], P('vir', 'occ'), may hold values from 0 to 1, as said below
Outputs:
- cycle: bfloat16 [512, 2048], P(('occ', 'vir'))
The draws below stay inside these ranges and needn't reach their ends.
Inputs may be any that keep to these rules, and one draw needn't show every extreme that they name: screen[a, k, t] is 1 where the amplitudes of first virtual a, occupied k and virtual tile t (virtuals t * 64 to (t + 1) * 64 - 1) survive screening, else 0.
All inputs are finite; a program needn't handle non-finite values.
Results may differ from the reference program's by a relative error of at most 0.001.
Values may be sent and summed in bfloat16 or wider, within the bound.
No kernel may reach another device: no remote copies, remote signals or barrier semaphores. Data moves between devices by JAX's collectives and lax.ppermute only.
A program may use at most 192 MiB of HBM per device.

```python
import jax
import jax.numpy as jnp
from jax import lax

TILE = 64
NI = 64
NJ = 64
NK = 64
NV = 4096
SB = 32
SA = 8


def draw_screen(key, part):
    key = jax.random.fold_in(key, 5)
    tile_count = NV // TILE
    density = 90 - 60 * jnp.arange(tile_count, dtype=jnp.int32) // max(tile_count - 1, 1)
    chance = jax.random.randint(key, (SA, NK, tile_count), 0, 100)
    return (chance < density[None, None, :]).astype(jnp.int32)


def with_spikes(drawn, own_key, source, target, parts, factor):
    owner, partner = [(jnp.arange(drawn.shape[axis_at]) // (drawn.shape[axis_at] // parts)).reshape([-1 if axis == axis_at else 1 for axis in range(drawn.ndim)]) for axis_at in (source, target)]
    chosen = jax.random.permutation(own_key, parts)[partner]
    strong = (owner == chosen) | (owner == (partner + parts // 2) % parts)
    return jnp.where(strong, factor * drawn, drawn)


def block_levels(key, dims, cuts, least, top_value):
    factor_of = 1.0
    for axis_at, shards_of in cuts:
        draws = jax.random.uniform(jax.random.fold_in(jax.random.fold_in(key, 6), axis_at), (shards_of,), jnp.float32, least / len(cuts), top_value / len(cuts))
        factor_of = factor_of * jnp.repeat(jnp.exp(draws), dims[axis_at] // shards_of).reshape((-1,) + (1,) * (len(dims) - 1 - axis_at))
    return factor_of


def noise(own_key, dims, spread, most, split=(), kind=jnp.bfloat16):
    drawn = spread * jax.random.normal(own_key, dims, jnp.float32)
    if split:
        drawn = drawn * block_levels(own_key, dims, split, -0.22, 0.18)
    return jnp.clip(drawn, -most, most).astype(kind)


def bell_draw_with(rng, dims, deviation, reach, cuts, heavy, kind=jnp.bfloat16):
    array = deviation * jax.random.normal(rng, dims, jnp.float32)
    if cuts:
        array = array * block_levels(rng, dims, cuts, -0.22, 0.18)
    return jnp.clip(with_spikes(array, jax.random.fold_in(rng, 3), *heavy), -reach, reach).astype(kind)


def setup_inputs(seed: int = 0) -> dict:
    streams_of = jax.random.split(jax.random.key(seed), 4)
    amplitudes = bell_draw_with(streams_of[0], (NI, SA, NK, NV), 1.0, 6.0, ((1, 8), (2, 4)), (3, 1, 8, 2.0))
    integrals = noise(streams_of[1], (NJ, SB, NK, NV), (NK * NV) ** -0.5, 0.01171875, ((2, 4), (3, 8)))
    screen = draw_screen(jax.random.fold_in(streams_of[3], 71), 0)
    return dict(amplitudes=amplitudes, integrals=integrals, screen=screen)


def reference(amplitudes, integrals, screen):
    keep_mask = jnp.repeat(screen, TILE, axis=2).astype(jnp.bfloat16)
    screened = amplitudes * keep_mask[None]
    left_rows = screened.reshape(NI * SA, NK * NV)
    right_rows = integrals.reshape(NJ * SB, NK * NV)
    product = lax.dot_general(left_rows, right_rows, (((1,), (1,)), ((), ())), preferred_element_type=jnp.float32)
    return product.astype(jnp.bfloat16)
```

```python
import jax
import jax.numpy as jnp
from jax import lax
from jax.experimental import pallas as pl
from jax.experimental.pallas import tpu as pltpu
from jax.sharding import PartitionSpec as P

TILE = 64
MIB = 1 << 20


def screen_kernel(amp_ref, screen_ref, out_ref):
    depth, width = amp_ref.shape[-2:]
    dest = pl.program_id(0)
    tiles = screen_ref.shape[-1]
    tile_at = lax.broadcasted_iota(jnp.int32, (tiles, width), 0)
    column = lax.broadcasted_iota(jnp.int32, (tiles, width), 1) + dest * width
    spread = (column // TILE == tile_at).astype(jnp.float32).astype(jnp.bfloat16)
    mask = jnp.dot(
        screen_ref[0].astype(jnp.float32).astype(jnp.bfloat16), spread, preferred_element_type=jnp.float32
    ).astype(jnp.bfloat16)
    block = amp_ref[...].reshape(-1, depth, width) * mask[None]
    out_ref[0] = jnp.swapaxes(block, 0, 1)


def screened_part(amplitudes, screen, part, n_occ, n_vir):
    depth, total = amplitudes.shape[2:]
    width = total // n_vir
    view = amplitudes.reshape(n_occ, n_vir // 2, 2, 2, depth, total)
    rows = n_occ * n_vir // 2
    return pl.pallas_call(
        screen_kernel,
        grid=(n_vir, 2),
        in_specs=[
            pl.BlockSpec((n_occ, n_vir // 2, 1, 1, depth, width), lambda d, c: (0, 0, c, part, 0, d)),
            pl.BlockSpec(screen.shape, lambda d, c: (0, 0, 0)),
        ],
        out_specs=pl.BlockSpec((1, depth, rows, width), lambda d, c: (d, 0, c, 0)),
        out_shape=jax.ShapeDtypeStruct((n_vir, depth, 2 * rows, width), jnp.bfloat16),
        compiler_params=pltpu.CompilerParams(vmem_limit_bytes=32 * MIB),
        name="screen_amplitudes",
    )(view, screen)


def product_kernel(left_ref, weight_ref, out_ref):
    sources, depth, rows, width = left_ref.shape
    total = None
    for k in range(depth):
        left = left_ref[:, k].reshape(sources * rows, width)
        term = lax.dot_general(
            left, weight_ref[k], (((1,), (1,)), ((), ())), preferred_element_type=jnp.float32
        )
        total = term if total is None else total + term
    half = rows // 2
    total = total.reshape(sources, 2, half, total.shape[-1])
    out_ref[0] = total[:, 0]
    out_ref[1] = total[:, 1]


def product(left, weights, block):
    sources, depth, rows, width = left.shape
    columns = weights.shape[1]
    return pl.pallas_call(
        product_kernel,
        grid=(columns // block,),
        in_specs=[
            pl.BlockSpec(left.shape, lambda n: (0, 0, 0, 0)),
            pl.BlockSpec((depth, block, width), lambda n: (0, n, 0)),
        ],
        out_specs=pl.BlockSpec((2, sources, rows // 2, block), lambda n: (0, 0, 0, n)),
        out_shape=jax.ShapeDtypeStruct((2, sources, rows // 2, columns), jnp.float32),
        compiler_params=pltpu.CompilerParams(vmem_limit_bytes=48 * MIB),
        cost_estimate=pl.CostEstimate(
            flops=2 * sources * rows * depth * width * columns,
            bytes_accessed=2 * (left.size + weights.size) + 4 * sources * rows * columns,
            transcendentals=0,
        ),
        name="product",
    )(left, weights)


def pick(x, at, axis):
    return lax.dynamic_index_in_dim(x, at, axis, keepdims=False)


def exchange(x, axis_name, step, size):
    return lax.ppermute(x, axis_name, [(j, j ^ step) for j in range(size)])


def owned(partial_sums, n_occ, n_vir):
    cores, firsts, _, columns = partial_sums.shape
    vir, occ = lax.axis_index("vir"), lax.axis_index("occ")
    core, z = vir % 2, vir // 2
    held = pick(partial_sums, core, 0) + exchange(pick(partial_sums, 1 - core, 0), "vir", 1, n_vir)
    n_z = n_vir // 2
    held = held.reshape(firsts, n_occ, n_z, columns)
    total = pick(held, occ, 1)
    for s in range(1, n_occ):
        total = total + exchange(pick(held, occ ^ s, 1), "occ", s, n_occ)
    held = total
    total = pick(held, z, 1)
    for s in range(1, n_z):
        total = total + exchange(pick(held, z ^ s, 1), "vir", 2 * s, n_vir)
    return total.astype(jnp.bfloat16)


def on_block(amplitudes, integrals, screen, n_occ, n_vir):
    columns = integrals.shape[0] * integrals.shape[1]
    weights = integrals.reshape(columns, *integrals.shape[2:]).swapaxes(0, 1)
    done = []
    for part in range(2):
        mine = screened_part(amplitudes, screen, part, n_occ, n_vir)
        left = lax.all_to_all(mine, "vir", 0, 0, tiled=True)
        done.append(owned(product(left, weights, 256), n_occ, n_vir))
    return jnp.stack(done).reshape(-1, columns)


def on_any(amplitudes, integrals, screen):
    keep_mask = jnp.repeat(screen, TILE, axis=2).astype(jnp.bfloat16)
    screened = amplitudes * keep_mask[None]
    columns = integrals.shape[0] * integrals.shape[1]
    flat_weights = integrals.reshape(columns, -1)
    relaid = lax.all_to_all(screened, "vir", split_axis=3, concat_axis=1, tiled=True)
    left_rows = relaid.reshape(-1, flat_weights.shape[1])
    partial_value = lax.dot_general(
        left_rows, flat_weights, (((1,), (1,)), ((), ())), preferred_element_type=jnp.float32
    )
    owned_rows = lax.psum_scatter(partial_value, ("occ", "vir"), scatter_dimension=0, tiled=True)
    return owned_rows.astype(jnp.bfloat16)


def solution(mesh):
    n_occ, n_vir = mesh.shape["occ"], mesh.shape["vir"]

    def on_device(amplitudes, integrals, screen):
        fits = n_occ == 4 and n_vir == 8
        if fits and amplitudes.shape[0] == 2 * n_occ * n_vir and amplitudes.shape[1] == 1:
            return on_block(amplitudes, integrals, screen, n_occ, n_vir)
        return on_any(amplitudes, integrals, screen)

    return jax.shard_map(
        on_device,
        mesh=mesh,
        in_specs=(P(None, "vir", "occ", None), P(None, None, "occ", "vir"), P("vir", "occ", None)),
        out_specs=P(("occ", "vir"), None),
        check_vma=False,
    )
```

```python
import functools

import jax
import jax.numpy as jnp
from jax import lax
from jax.experimental import pallas as pl
from jax.experimental.pallas import tpu as pltpu
from jax.sharding import PartitionSpec as P

TILE = 64
VMEM = 60 << 20


def screen_block(amp, screen_ref, dest):
    depth, width = amp.shape[-2:]
    tiles = screen_ref.shape[-1]
    tile_at = lax.broadcasted_iota(jnp.int32, (tiles, width), 0)
    column = lax.broadcasted_iota(jnp.int32, (tiles, width), 1) + dest * width
    spread = (column // TILE == tile_at).astype(jnp.float32).astype(jnp.bfloat16)
    rows = screen_ref[0].astype(jnp.float32).astype(jnp.bfloat16)
    mask = jnp.dot(rows, spread, preferred_element_type=jnp.float32).astype(jnp.bfloat16)
    return jnp.swapaxes(amp.reshape(-1, depth, width) * mask[None], 0, 1)


def screen_kernel(*refs, dests):
    screen_ref, out_ref = refs[dests], refs[-1]
    for dest in range(dests):
        out_ref[dest] = screen_block(refs[dest][...], screen_ref, dest)


def screened_part(amplitudes, screen, part, n_occ, n_vir):
    depth, total = amplitudes.shape[2:]
    width, rows = total // n_vir, n_occ * n_vir // 2
    view = amplitudes.reshape(n_occ, n_vir // 2, 2, 2, depth, total)
    some = depth // 2

    def source(dest):
        return pl.BlockSpec((n_occ, n_vir // 2, 1, 1, some, width), lambda c, k: (0, 0, c, part, k, dest))

    return pl.pallas_call(
        functools.partial(screen_kernel, dests=n_vir),
        grid=(2, 2),
        in_specs=[source(dest) for dest in range(n_vir)]
        + [pl.BlockSpec((1, some, screen.shape[2]), lambda c, k: (0, k, 0))],
        out_specs=pl.BlockSpec((n_vir, some, rows, width), lambda c, k: (0, k, c, 0)),
        out_shape=jax.ShapeDtypeStruct((n_vir, depth, 2 * rows, width), jnp.bfloat16),
        compiler_params=pltpu.CompilerParams(vmem_limit_bytes=VMEM),
        cost_estimate=pl.CostEstimate(flops=0, bytes_accessed=0, transcendentals=0),
        name="screen",
    )(*[view] * n_vir, screen)


def product_kernel(me_ref, left_ref, weight_ref, *refs):
    mine_ref, give_ref = refs[-2:]
    units, depth, rows, width = left_ref.shape
    piece = mine_ref.shape[1]
    total = None
    for k in range(depth):
        term = lax.dot_general(
            left_ref[:, k].reshape(units * rows, width),
            weight_ref[k],
            (((1,), (1,)), ((), ())),
            preferred_element_type=jnp.float32,
        )
        total = term if total is None else total + term
    odd = me_ref[0] % 2 == 1
    for unit in range(units):
        zero, one = (total[unit * rows + core * piece : unit * rows + (core + 1) * piece] for core in range(2))
        mine_ref[unit] = jnp.where(odd, one, zero)
        give_ref[unit] = jnp.where(odd, zero, one)


def product(left, weights, first, count, block, after=(), limit=VMEM, cost=0):
    units, depth, rows, width = left.shape
    out = jax.ShapeDtypeStruct((units, rows // 2, count), jnp.float32)
    out_spec = pl.BlockSpec((units, rows // 2, block), lambda n, at: (0, 0, n))
    return pl.pallas_call(
        product_kernel,
        grid_spec=pltpu.PrefetchScalarGridSpec(
            num_scalar_prefetch=1,
            grid=(count // block,),
            in_specs=[
                pl.BlockSpec(left.shape, lambda n, at: (0, 0, 0, 0)),
                pl.BlockSpec((depth, block, width), lambda n, at: (0, first // block + n, 0)),
                *[pl.BlockSpec(memory_space=pl.ANY) for _ in after],
            ],
            out_specs=[out_spec, out_spec],
        ),
        out_shape=[out, out],
        compiler_params=pltpu.CompilerParams(vmem_limit_bytes=limit),
        cost_estimate=pl.CostEstimate(flops=cost, bytes_accessed=0, transcendentals=0),
        name="product",
    )(lax.axis_index("vir").astype(jnp.int32).reshape(1), left, weights, *after)


def pick(x, at, axis):
    return lax.dynamic_index_in_dim(x, at, axis, keepdims=False)


def exchange(x, axis_name, step, size):
    return lax.ppermute(x, axis_name, [(j, j ^ step) for j in range(size)])


def in_plane(mine, give, n_occ, n_vir):
    occ, n_z = lax.axis_index("occ"), n_vir // 2
    held = mine + exchange(give, "vir", 1, n_vir)
    held = held.reshape(held.shape[0], n_occ, n_z, held.shape[-1])
    total = pick(held, occ, 1)
    for s in range(1, n_occ):
        total = total + exchange(pick(held, occ ^ s, 1), "occ", s, n_occ)
    return total


def along_z(total, n_vir):
    z, n_z = lax.axis_index("vir") // 2, n_vir // 2
    out = pick(total, z, 1)
    for s in range(1, n_z):
        out = out + exchange(pick(total, z ^ s, 1), "vir", 2 * s, n_vir)
    return out


def on_block(amplitudes, integrals, screen, n_occ, n_vir):
    columns = integrals.shape[0] * integrals.shape[1]
    weights = integrals.reshape(columns, *integrals.shape[2:]).swapaxes(0, 1)
    cuts = 1
    count = columns // cuts
    left = [
        lax.all_to_all(screened_part(amplitudes, screen, part, n_occ, n_vir), "vir", 0, 0, tiled=True)
        for part in range(2)
    ]
    first = in_plane(*product(left[0], weights, 0, columns, 512), n_occ, n_vir)
    last, after = [], (first,)
    for cut in range(cuts):
        mine, give = product(left[1], weights, cut * count, count, 512, after, limit=VMEM, cost=0)
        after = (first, give)
        last.append(in_plane(mine, give, n_occ, n_vir))
    last = [along_z(x, n_vir) for x in last]
    done = jnp.stack([along_z(first, n_vir), jnp.concatenate(last, axis=1)])
    return done.astype(jnp.bfloat16).reshape(-1, columns)


def on_any(amplitudes, integrals, screen):
    keep_mask = jnp.repeat(screen, TILE, axis=2).astype(jnp.bfloat16)
    screened = amplitudes * keep_mask[None]
    columns = integrals.shape[0] * integrals.shape[1]
    flat_weights = integrals.reshape(columns, -1)
    relaid = lax.all_to_all(screened, "vir", split_axis=3, concat_axis=1, tiled=True)
    left_rows = relaid.reshape(-1, flat_weights.shape[1])
    partial_value = lax.dot_general(
        left_rows, flat_weights, (((1,), (1,)), ((), ())), preferred_element_type=jnp.float32
    )
    owned_rows = lax.psum_scatter(partial_value, ("occ", "vir"), scatter_dimension=0, tiled=True)
    return owned_rows.astype(jnp.bfloat16)


def solution(mesh):
    n_occ, n_vir = mesh.shape["occ"], mesh.shape["vir"]

    def on_device(amplitudes, integrals, screen):
        fits = n_occ == 4 and n_vir == 8
        if fits and amplitudes.shape[0] == 2 * n_occ * n_vir and amplitudes.shape[1] == 1:
            return on_block(amplitudes, integrals, screen, n_occ, n_vir)
        return on_any(amplitudes, integrals, screen)

    return jax.shard_map(
        on_device,
        mesh=mesh,
        in_specs=(P(None, "vir", "occ", None), P(None, None, "occ", "vir"), P("vir", "occ", None)),
        out_specs=P(("occ", "vir"), None),
        check_vma=False,
    )
```

```python
import functools

import jax
import jax.numpy as jnp
from jax import lax
from jax.experimental import pallas as pl
from jax.experimental.pallas import tpu as pltpu
from jax.sharding import PartitionSpec as P

TILE = 64
VMEM = 60 << 20


def screen_block(amp, screen_ref, dest):
    depth, width = amp.shape[-2:]
    tiles = screen_ref.shape[-1]
    tile_at = lax.broadcasted_iota(jnp.int32, (tiles, width), 0)
    column = lax.broadcasted_iota(jnp.int32, (tiles, width), 1) + dest * width
    spread = (column // TILE == tile_at).astype(jnp.float32).astype(jnp.bfloat16)
    rows = screen_ref[0].astype(jnp.float32).astype(jnp.bfloat16)
    mask = jnp.dot(rows, spread, preferred_element_type=jnp.float32).astype(jnp.bfloat16)
    return jnp.swapaxes(amp.reshape(-1, depth, width) * mask[None], 0, 1)


def give_kernel(me_ref, amp_ref, screen_ref, *refs, steps):
    out_ref = refs[-1]
    step = steps[0]
    for at, other in enumerate(steps):
        step = jnp.where(pl.program_id(0) == at, other, step)
    out_ref[0] = screen_block(amp_ref[...], screen_ref, me_ref[0] ^ (2 * step + 1))


def keep_kernel(me_ref, *refs, steps, parts):
    screen_ref, given_refs = refs[len(steps)], refs[len(steps) + 1 : 2 * len(steps) + 1]
    out_refs = refs[len(refs) - len(steps) :]
    for at, step in enumerate(steps):
        out_refs[at][0] = screen_block(refs[at][...], screen_ref, me_ref[0] ^ (2 * step))
        out_refs[at][1] = given_refs[at][0]


def position():
    return lax.axis_index("vir").astype(jnp.int32).reshape(1)


def amplitude_view(amplitudes, n_occ, n_vir):
    return amplitudes.reshape(n_occ, n_vir // 2, 2, 2, *amplitudes.shape[2:])


def given(amplitudes, screen, units, n_occ, n_vir, after=()):
    depth, total = amplitudes.shape[2:]
    width, rows = total // n_vir, n_occ * n_vir // 2
    parts, steps = [u[0] for u in units], [u[1] for u in units]

    def choose(values, at):
        out = values[0]
        for n, value in enumerate(values):
            out = jnp.where(at == n, value, out)
        return out

    return pl.pallas_call(
        functools.partial(give_kernel, steps=steps),
        grid_spec=pltpu.PrefetchScalarGridSpec(
            num_scalar_prefetch=1,
            grid=(len(units), 2),
            in_specs=[
                pl.BlockSpec(
                    (n_occ, n_vir // 2, 1, 1, depth, width),
                    lambda u, c, at: (0, 0, c, choose(parts, u), 0, at[0] ^ (2 * choose(steps, u) + 1)),
                ),
                pl.BlockSpec(screen.shape, lambda u, c, at: (0, 0, 0)),
            ]
            + [pl.BlockSpec(memory_space=pl.ANY) for _ in after],
            out_specs=pl.BlockSpec((1, depth, rows, width), lambda u, c, at: (u, 0, c, 0)),
        ),
        out_shape=jax.ShapeDtypeStruct((len(units), depth, 2 * rows, width), jnp.bfloat16),
        compiler_params=pltpu.CompilerParams(vmem_limit_bytes=VMEM),
        cost_estimate=pl.CostEstimate(flops=0, bytes_accessed=0, transcendentals=0),
        name="give",
    )(position(), amplitude_view(amplitudes, n_occ, n_vir), screen, *after)


def kept(amplitudes, screen, got, first, parts, steps, base, n_occ, n_vir, after=()):
    depth, total = amplitudes.shape[2:]
    width, rows = total // n_vir, n_occ * n_vir // 2
    view = amplitude_view(amplitudes, n_occ, n_vir)

    def source(step):
        return pl.BlockSpec(
            (n_occ, n_vir // 2, 1, 1, depth, width), lambda p, c, at: (0, 0, c, first + p, 0, at[0] ^ (2 * step))
        )

    def sibling(n):
        return pl.BlockSpec((1, depth, rows, width), lambda p, c, at: (base + n * parts + p, 0, c, 0))

    return pl.pallas_call(
        functools.partial(keep_kernel, steps=steps, parts=parts),
        grid_spec=pltpu.PrefetchScalarGridSpec(
            num_scalar_prefetch=1,
            grid=(parts, 2),
            in_specs=[source(step) for step in steps]
            + [pl.BlockSpec(screen.shape, lambda p, c, at: (0, 0, 0))]
            + [sibling(n) for n in range(len(steps))]
            + [pl.BlockSpec(memory_space=pl.ANY) for _ in after],
            out_specs=[pl.BlockSpec((2, depth, rows, width), lambda p, c, at: (p, 0, c, 0)) for _ in steps],
        ),
        out_shape=[jax.ShapeDtypeStruct((2 * parts, depth, 2 * rows, width), jnp.bfloat16) for _ in steps],
        compiler_params=pltpu.CompilerParams(vmem_limit_bytes=VMEM),
        cost_estimate=pl.CostEstimate(flops=0, bytes_accessed=0, transcendentals=0),
        name="keep",
    )(position(), *[view] * len(steps), screen, *[got] * len(steps), *after)


def screen_kernel(*refs, dests):
    screen_ref, out_ref = refs[-2:]
    width = out_ref.shape[-1]
    per = screen_ref.shape[-1] // dests
    tile_at = lax.broadcasted_iota(jnp.int32, (per, width), 0)
    column = lax.broadcasted_iota(jnp.int32, (per, width), 1)
    spread = (column // TILE == tile_at).astype(jnp.float32).astype(jnp.bfloat16)
    rows = screen_ref[0].astype(jnp.float32).astype(jnp.bfloat16)
    for dest in range(dests):
        mask = jnp.dot(rows[:, dest * per : (dest + 1) * per], spread, preferred_element_type=jnp.float32)
        mask = mask.astype(jnp.bfloat16)[None]
        for core in range(2):
            block = refs[dest][:, :, core, 0]
            block = block.reshape(-1, *block.shape[2:])
            count = block.shape[0]
            out_ref[dest, :, core * count : (core + 1) * count] = jnp.swapaxes(block * mask, 0, 1)


def screened(amplitudes, screen, n_occ, n_vir):
    depth, total = amplitudes.shape[2:]
    width, n_z = total // n_vir, n_vir // 2
    some, rows = depth // 2, n_occ * n_vir

    def source(dest):
        return pl.BlockSpec((n_occ, n_z, 2, 1, some, width), lambda k: (0, 0, 0, 0, k, dest))

    return pl.pallas_call(
        functools.partial(screen_kernel, dests=n_vir),
        grid=(2,),
        in_specs=[source(dest) for dest in range(n_vir)]
        + [pl.BlockSpec((1, some, screen.shape[2]), lambda k: (0, k, 0))],
        out_specs=pl.BlockSpec((n_vir, some, rows, width), lambda k: (0, k, 0, 0)),
        out_shape=jax.ShapeDtypeStruct((n_vir, depth, rows, width), jnp.bfloat16),
        compiler_params=pltpu.CompilerParams(vmem_limit_bytes=VMEM),
        cost_estimate=pl.CostEstimate(flops=0, bytes_accessed=0, transcendentals=0),
        name="screen",
    )(*[amplitude_view(amplitudes, n_occ, n_vir)] * n_vir, screen)


def gate_kernel(*refs):
    del refs


def held_back(arrays, after):
    return pl.pallas_call(
        gate_kernel,
        in_specs=[pl.BlockSpec(memory_space=pl.ANY)] * (len(arrays) + len(after)),
        out_specs=[pl.BlockSpec(memory_space=pl.ANY)] * len(arrays),
        out_shape=[jax.ShapeDtypeStruct(x.shape, x.dtype) for x in arrays],
        input_output_aliases={n: n for n in range(len(arrays))},
        cost_estimate=pl.CostEstimate(flops=0, bytes_accessed=0, transcendentals=0),
        name="gate",
    )(*arrays, *after)


def product_kernel(me_ref, *refs, count, plain):
    left_refs, weight_ref, mine_ref, give_ref = refs[:count], refs[count], refs[-2], refs[-1]
    piece = mine_ref.shape[1]
    total = None
    for k in range(weight_ref.shape[0]):
        left = [ref[unit, k] for ref in left_refs for unit in range(ref.shape[0])]
        term = lax.dot_general(
            jnp.concatenate(left, axis=0),
            weight_ref[k],
            (((1,), (1,)), ((), ())),
            preferred_element_type=jnp.float32,
        )
        total = term if total is None else total + term
    odd = me_ref[0] % 2 == 1
    for unit in range(mine_ref.shape[0]):
        zero, one = (total[(2 * unit + core) * piece : (2 * unit + core + 1) * piece] for core in range(2))
        mine_ref[unit] = jnp.where(odd, one, zero)
        give_ref[unit if unit < plain else unit ^ 1] = jnp.where(odd, zero, one)


def product(lefts, weights, block, plain, turn=0, after=()):
    columns = weights.shape[1]
    shape = (sum(x.shape[0] for x in lefts), lefts[0].shape[2] // 2, columns)
    out_spec = pl.BlockSpec((*shape[:-1], block), lambda n, at: (0, 0, n))
    return pl.pallas_call(
        functools.partial(product_kernel, count=len(lefts), plain=plain),
        grid_spec=pltpu.PrefetchScalarGridSpec(
            num_scalar_prefetch=1,
            grid=(columns // block,),
            in_specs=[pl.BlockSpec(x.shape, lambda n, at: (0, 0, 0, 0)) for x in lefts]
            + [pl.BlockSpec((weights.shape[0], block, weights.shape[2]), lambda n, at: (0, n, 0))]
            + [pl.BlockSpec(memory_space=pl.ANY) for _ in after],
            out_specs=[out_spec, out_spec],
        ),
        out_shape=[jax.ShapeDtypeStruct(shape, jnp.float32)] * 2,
        compiler_params=pltpu.CompilerParams(vmem_limit_bytes=VMEM),
        cost_estimate=pl.CostEstimate(flops=0, bytes_accessed=0, transcendentals=0),
        name="product",
    )(position() + 2 * turn, *lefts, weights, *after)


def pick(x, at, axis):
    return lax.dynamic_index_in_dim(x, at, axis, keepdims=False)


def exchange(x, axis_name, step, size):
    return lax.ppermute(x, axis_name, [(j, j ^ step) for j in range(size)])


def over_cores(mine, give, n_occ, n_vir):
    held = mine + exchange(give, "vir", 1, n_vir)
    return held.reshape(held.shape[0], n_occ, n_vir // 2, held.shape[-1])


def over_plane(held, n_occ):
    occ = lax.axis_index("occ")
    total = pick(held, occ, 1)
    for s in range(1, n_occ):
        total = total + exchange(pick(held, occ ^ s, 1), "occ", s, n_occ)
    return total


def in_turn(held, index, axis_name, unit, size):
    step, count = 1, held.shape[1]
    while step < count:
        bit = (index // step) % 2
        parts = held.reshape(held.shape[0], -1, 2, *held.shape[2:])
        held = pick(parts, bit, 2) + exchange(pick(parts, 1 - bit, 2), axis_name, unit * step, size)
        step *= 2
    return held[:, 0]


def combine_kernel(me_ref, *refs, firsts):
    out_ref = refs[-1]
    n_z = len(refs) // 2
    plain = total = None
    for s in range(n_z):
        early = refs[s][...]
        value = jnp.concatenate([early[firsts:], refs[n_z + s][...]], axis=0)
        term = jnp.concatenate([value[m ^ 2 * s :][:1] for m in range(firsts)], axis=0) if s else value
        plain = plain + early[:firsts] if s else early[:firsts]
        total = total + term if s else term
    bit = 1
    while bit < firsts:
        other = jnp.concatenate([total[m ^ bit :][:1] for m in range(firsts)], axis=0)
        total = jnp.where((me_ref[0] & bit) != 0, other, total)
        bit *= 2
    out_ref[...] = jnp.concatenate([plain, total], axis=0).astype(out_ref.dtype)


def combined(early, late):
    columns = early[0].shape[1]
    firsts = (early[0].shape[0] + late[0].shape[0]) // 2
    block = columns // 2
    return pl.pallas_call(
        functools.partial(combine_kernel, firsts=firsts),
        grid_spec=pltpu.PrefetchScalarGridSpec(
            num_scalar_prefetch=1,
            grid=(columns // block,),
            in_specs=[pl.BlockSpec((x.shape[0], block), lambda n, at: (0, n)) for x in (*early, *late)],
            out_specs=pl.BlockSpec((2 * firsts, block), lambda n, at: (0, n)),
        ),
        out_shape=jax.ShapeDtypeStruct((2 * firsts, columns), jnp.bfloat16),
        name="combine",
    )(position(), *early, *late)


def along_z(sums, n_vir):
    z = lax.axis_index("vir") // 2
    return [pick(sums, z, 1)] + [exchange(pick(sums, z ^ s, 1), "vir", 2 * s, n_vir) for s in range(1, n_vir // 2)]


def on_block(amplitudes, integrals, screen, n_occ, n_vir):
    columns = integrals.shape[0] * integrals.shape[1]
    weights = integrals.reshape(columns, *integrals.shape[2:]).swapaxes(0, 1)
    n_z = n_vir // 2
    occ = lax.axis_index("occ")
    steps = list(range(n_z))
    soon, later = steps[:2], steps[2:]
    first = lax.all_to_all(screened(amplitudes, screen, n_occ, n_vir), "vir", 0, 0, tiled=True)

    give = given(amplitudes, screen, [(1, s) for s in steps], n_occ, n_vir, after=(weights,))
    got = exchange(give, "vir", 1, n_vir)
    last = []
    if soon:
        last += kept(amplitudes, screen, got, 1, 1, soon, 0, n_occ, n_vir)
    last += held_back(kept(amplitudes, screen, got, 1, 1, later, len(soon), n_occ, n_vir), (first,))
    last = [x if s == 0 else exchange(x, "vir", 2 * s, n_vir) for s, x in zip(steps, last)]

    def early(turn, _):
        held = over_cores(*product([first, *last[: len(soon)]], weights, 512, n_vir, turn), n_occ, n_vir)
        return in_turn(held, occ, "occ", 1, n_occ)

    once = 1 + lax.axis_index("vir") // n_vir
    units = n_vir + 2 * len(soon)
    early_sums = lax.fori_loop(0, once, early, jnp.zeros((units, n_z, columns), jnp.float32))
    mine, give = product(last[len(soon) :], weights, 512, 0, after=(early_sums,))
    late_sums = over_plane(over_cores(mine, give, n_occ, n_vir), n_occ)
    return combined(along_z(early_sums, n_vir), along_z(late_sums, n_vir))


def on_any(amplitudes, integrals, screen):
    keep_mask = jnp.repeat(screen, TILE, axis=2).astype(jnp.bfloat16)
    screened = amplitudes * keep_mask[None]
    columns = integrals.shape[0] * integrals.shape[1]
    flat_weights = integrals.reshape(columns, -1)
    relaid = lax.all_to_all(screened, "vir", split_axis=3, concat_axis=1, tiled=True)
    left_rows = relaid.reshape(-1, flat_weights.shape[1])
    partial_value = lax.dot_general(
        left_rows, flat_weights, (((1,), (1,)), ((), ())), preferred_element_type=jnp.float32
    )
    owned_rows = lax.psum_scatter(partial_value, ("occ", "vir"), scatter_dimension=0, tiled=True)
    return owned_rows.astype(jnp.bfloat16)


def solution(mesh):
    n_occ, n_vir = mesh.shape["occ"], mesh.shape["vir"]

    def on_device(amplitudes, integrals, screen):
        fits = n_occ == 4 and n_vir == 8
        if fits and amplitudes.shape[0] == 2 * n_occ * n_vir and amplitudes.shape[1] == 1:
            return on_block(amplitudes, integrals, screen, n_occ, n_vir)
        return on_any(amplitudes, integrals, screen)

    return jax.shard_map(
        on_device,
        mesh=mesh,
        in_specs=(P(None, "vir", "occ", None), P(None, None, "occ", "vir"), P("vir", "occ", None)),
        out_specs=P(("occ", "vir"), None),
        check_vma=False,
    )
```

```python
import functools

import jax
import jax.numpy as jnp
from jax import lax
from jax.experimental import pallas as pl
from jax.experimental.pallas import tpu as pltpu
from jax.sharding import PartitionSpec as P

TILE = 64
VMEM = 60 << 20
HELD = 12 << 20


def screen_block(amp, screen_ref, dest):
    depth, width = amp.shape[-2:]
    tiles = screen_ref.shape[-1]
    tile_at = lax.broadcasted_iota(jnp.int32, (tiles, width), 0)
    column = lax.broadcasted_iota(jnp.int32, (tiles, width), 1) + dest * width
    spread = (column // TILE == tile_at).astype(jnp.float32).astype(jnp.bfloat16)
    rows = screen_ref[0].astype(jnp.float32).astype(jnp.bfloat16)
    mask = jnp.dot(rows, spread, preferred_element_type=jnp.float32).astype(jnp.bfloat16)
    return jnp.swapaxes(amp.reshape(-1, depth, width) * mask[None], 0, 1)


def give_kernel(me_ref, amp_ref, screen_ref, *refs, steps):
    out_ref = refs[-1]
    step = steps[0]
    for at, other in enumerate(steps):
        step = jnp.where(pl.program_id(0) == at, other, step)
    out_ref[0] = screen_block(amp_ref[...], screen_ref, me_ref[0] ^ (2 * step + 1))


def keep_kernel(me_ref, *refs, steps, parts):
    screen_ref, given_refs = refs[len(steps)], refs[len(steps) + 1 : 2 * len(steps) + 1]
    out_refs = refs[len(refs) - len(steps) :]
    for at, step in enumerate(steps):
        out_refs[at][0] = screen_block(refs[at][...], screen_ref, me_ref[0] ^ (2 * step))
        out_refs[at][1] = given_refs[at][0]


def position():
    return lax.axis_index("vir").astype(jnp.int32).reshape(1)


def amplitude_view(amplitudes, n_occ, n_vir):
    return amplitudes.reshape(n_occ, n_vir // 2, 2, 2, *amplitudes.shape[2:])


def given(amplitudes, screen, units, n_occ, n_vir, after=()):
    depth, total = amplitudes.shape[2:]
    width, rows = total // n_vir, n_occ * n_vir // 2
    parts, steps = [u[0] for u in units], [u[1] for u in units]

    def choose(values, at):
        out = values[0]
        for n, value in enumerate(values):
            out = jnp.where(at == n, value, out)
        return out

    return pl.pallas_call(
        functools.partial(give_kernel, steps=steps),
        grid_spec=pltpu.PrefetchScalarGridSpec(
            num_scalar_prefetch=1,
            grid=(len(units), 2),
            in_specs=[
                pl.BlockSpec(
                    (n_occ, n_vir // 2, 1, 1, depth, width),
                    lambda u, c, at: (0, 0, c, choose(parts, u), 0, at[0] ^ (2 * choose(steps, u) + 1)),
                ),
                pl.BlockSpec(screen.shape, lambda u, c, at: (0, 0, 0)),
            ]
            + [pl.BlockSpec(memory_space=pl.ANY) for _ in after],
            out_specs=pl.BlockSpec((1, depth, rows, width), lambda u, c, at: (u, 0, c, 0)),
        ),
        out_shape=jax.ShapeDtypeStruct((len(units), depth, 2 * rows, width), jnp.bfloat16),
        compiler_params=pltpu.CompilerParams(vmem_limit_bytes=VMEM),
        cost_estimate=pl.CostEstimate(flops=0, bytes_accessed=0, transcendentals=0),
        name="give",
    )(position(), amplitude_view(amplitudes, n_occ, n_vir), screen, *after)


def kept(amplitudes, screen, got, first, parts, steps, base, n_occ, n_vir, after=()):
    depth, total = amplitudes.shape[2:]
    width, rows = total // n_vir, n_occ * n_vir // 2
    view = amplitude_view(amplitudes, n_occ, n_vir)

    def source(step):
        return pl.BlockSpec(
            (n_occ, n_vir // 2, 1, 1, depth, width), lambda p, c, at: (0, 0, c, first + p, 0, at[0] ^ (2 * step))
        )

    def sibling(n):
        return pl.BlockSpec((1, depth, rows, width), lambda p, c, at: (base + n * parts + p, 0, c, 0))

    return pl.pallas_call(
        functools.partial(keep_kernel, steps=steps, parts=parts),
        grid_spec=pltpu.PrefetchScalarGridSpec(
            num_scalar_prefetch=1,
            grid=(parts, 2),
            in_specs=[source(step) for step in steps]
            + [pl.BlockSpec(screen.shape, lambda p, c, at: (0, 0, 0))]
            + [sibling(n) for n in range(len(steps))]
            + [pl.BlockSpec(memory_space=pl.ANY) for _ in after],
            out_specs=[pl.BlockSpec((2, depth, rows, width), lambda p, c, at: (p, 0, c, 0)) for _ in steps],
        ),
        out_shape=[jax.ShapeDtypeStruct((2 * parts, depth, 2 * rows, width), jnp.bfloat16) for _ in steps],
        compiler_params=pltpu.CompilerParams(vmem_limit_bytes=VMEM),
        cost_estimate=pl.CostEstimate(flops=0, bytes_accessed=0, transcendentals=0),
        name="keep",
    )(position(), *[view] * len(steps), screen, *[got] * len(steps), *after)


def screen_kernel(*refs, dests):
    screen_ref, out_ref = refs[-2:]
    width = out_ref.shape[-1]
    per = screen_ref.shape[-1] // dests
    tile_at = lax.broadcasted_iota(jnp.int32, (per, width), 0)
    column = lax.broadcasted_iota(jnp.int32, (per, width), 1)
    spread = (column // TILE == tile_at).astype(jnp.float32).astype(jnp.bfloat16)
    rows = screen_ref[0].astype(jnp.float32).astype(jnp.bfloat16)
    for dest in range(dests):
        mask = jnp.dot(rows[:, dest * per : (dest + 1) * per], spread, preferred_element_type=jnp.float32)
        mask = mask.astype(jnp.bfloat16)[None]
        for core in range(2):
            block = refs[dest][:, :, core, 0]
            block = block.reshape(-1, *block.shape[2:])
            count = block.shape[0]
            out_ref[dest, :, core * count : (core + 1) * count] = jnp.swapaxes(block * mask, 0, 1)


def screened(amplitudes, screen, n_occ, n_vir):
    depth, total = amplitudes.shape[2:]
    width, n_z = total // n_vir, n_vir // 2
    some, rows = depth // 2, n_occ * n_vir

    def source(dest):
        return pl.BlockSpec((n_occ, n_z, 2, 1, some, width), lambda k: (0, 0, 0, 0, k, dest))

    return pl.pallas_call(
        functools.partial(screen_kernel, dests=n_vir),
        grid=(2,),
        in_specs=[source(dest) for dest in range(n_vir)]
        + [pl.BlockSpec((1, some, screen.shape[2]), lambda k: (0, k, 0))],
        out_specs=pl.BlockSpec((n_vir, some, rows, width), lambda k: (0, k, 0, 0)),
        out_shape=jax.ShapeDtypeStruct((n_vir, depth, rows, width), jnp.bfloat16),
        compiler_params=pltpu.CompilerParams(vmem_limit_bytes=VMEM),
        cost_estimate=pl.CostEstimate(flops=0, bytes_accessed=0, transcendentals=0),
        name="screen",
    )(*[amplitude_view(amplitudes, n_occ, n_vir)] * n_vir, screen)


def gate_kernel(*refs):
    del refs


def held_back(arrays, after):
    return pl.pallas_call(
        gate_kernel,
        in_specs=[pl.BlockSpec(memory_space=pl.ANY)] * (len(arrays) + len(after)),
        out_specs=[pl.BlockSpec(memory_space=pl.ANY)] * len(arrays),
        out_shape=[jax.ShapeDtypeStruct(x.shape, x.dtype) for x in arrays],
        input_output_aliases={n: n for n in range(len(arrays))},
        cost_estimate=pl.CostEstimate(flops=0, bytes_accessed=0, transcendentals=0),
        name="gate",
    )(*arrays, *after)


def product_kernel(me_ref, *refs, count, plain):
    left_refs, weight_ref, mine_ref, give_ref = refs[:count], refs[count], refs[-2], refs[-1]
    piece = mine_ref.shape[1]
    total = None
    for k in range(weight_ref.shape[0]):
        left = [ref[unit, k] for ref in left_refs for unit in range(ref.shape[0])]
        term = lax.dot_general(
            jnp.concatenate(left, axis=0),
            weight_ref[k],
            (((1,), (1,)), ((), ())),
            preferred_element_type=jnp.float32,
        )
        total = term if total is None else total + term
    odd = me_ref[0] % 2 == 1
    for unit in range(mine_ref.shape[0]):
        zero, one = (total[(2 * unit + core) * piece : (2 * unit + core + 1) * piece] for core in range(2))
        mine_ref[unit] = jnp.where(odd, one, zero)
        give_ref[unit if unit < plain else unit ^ 1] = jnp.where(odd, zero, one)


def product(lefts, weights, block, plain, turn=0, after=()):
    columns = weights.shape[1]
    shape = (sum(x.shape[0] for x in lefts), lefts[0].shape[2] // 2, columns)
    out_spec = pl.BlockSpec((*shape[:-1], block), lambda n, at: (0, 0, n))
    return pl.pallas_call(
        functools.partial(product_kernel, count=len(lefts), plain=plain),
        grid_spec=pltpu.PrefetchScalarGridSpec(
            num_scalar_prefetch=1,
            grid=(columns // block,),
            in_specs=[pl.BlockSpec(x.shape, lambda n, at: (0, 0, 0, 0)) for x in lefts]
            + [pl.BlockSpec((weights.shape[0], block, weights.shape[2]), lambda n, at: (0, n, 0))]
            + [pl.BlockSpec(memory_space=pl.ANY) for _ in after],
            out_specs=[out_spec, out_spec],
        ),
        out_shape=[jax.ShapeDtypeStruct(shape, jnp.float32)] * 2,
        compiler_params=pltpu.CompilerParams(vmem_limit_bytes=VMEM),
        cost_estimate=pl.CostEstimate(flops=0, bytes_accessed=0, transcendentals=0),
        name="product",
    )(position() + 2 * turn, *lefts, weights, *after)


def hold_kernel(weight_ref, *refs):
    out_ref, sems = refs[-2:]
    copies = [
        pltpu.make_async_copy(weight_ref.at[k], out_ref.at[k], sems.at[k]) for k in range(weight_ref.shape[0])
    ]
    for copy in copies:
        copy.start()
    for copy in copies:
        copy.wait()


def held_in_vmem(weights, after):
    return pl.pallas_call(
        hold_kernel,
        in_specs=[pl.BlockSpec(memory_space=pl.ANY)] * (1 + len(after)),
        out_specs=pl.BlockSpec(memory_space=pltpu.VMEM),
        out_shape=pltpu.VMEM(weights.shape, weights.dtype),
        scratch_shapes=[pltpu.SemaphoreType.DMA((weights.shape[0],))],
        compiler_params=pltpu.CompilerParams(vmem_limit_bytes=1 << 20),
        cost_estimate=pl.CostEstimate(flops=0, bytes_accessed=0, transcendentals=0),
        name="hold",
    )(weights, *after)


def held_product_kernel(*refs, block, turned):
    *left_refs, weight_ref, mine_ref, give_ref = refs
    piece, columns = mine_ref.shape[1:]
    odd = lax.axis_index("vir") % 2 == 1

    @pl.loop(0, columns // block)
    def _(n):
        at = pl.multiple_of(n * block, block)
        total = None
        for k in range(weight_ref.shape[0]):
            left = jnp.concatenate([ref[unit, k] for ref in left_refs for unit in range(ref.shape[0])], axis=0)
            weight = weight_ref[k, pl.ds(at, block)]
            term = lax.dot_general(
                *((weight, left) if turned else (left, weight)),
                (((1,), (1,)), ((), ())),
                preferred_element_type=jnp.float32,
            )
            total = term if total is None else total + term
        if turned:
            total = total.T
        for unit in range(mine_ref.shape[0]):
            zero, one = (total[(2 * unit + core) * piece : (2 * unit + core + 1) * piece] for core in range(2))
            mine_ref[unit, :, pl.ds(at, block)] = jnp.where(odd, one, zero)
            give_ref[unit ^ 1, :, pl.ds(at, block)] = jnp.where(odd, zero, one)


def held_product(lefts, weights, block, turned):
    shape = (sum(x.shape[0] for x in lefts), lefts[0].shape[2] // 2, weights.shape[1])
    return pl.pallas_call(
        functools.partial(held_product_kernel, block=block, turned=turned),
        in_specs=[pl.BlockSpec(memory_space=pltpu.VMEM)] * (1 + len(lefts)),
        out_specs=[pl.BlockSpec(memory_space=pltpu.VMEM)] * 2,
        out_shape=[jax.ShapeDtypeStruct(shape, jnp.float32)] * 2,
        compiler_params=pltpu.CompilerParams(vmem_limit_bytes=HELD),
        cost_estimate=pl.CostEstimate(flops=0, bytes_accessed=0, transcendentals=0),
        name="product_held",
    )(*lefts, weights)


def pick(x, at, axis):
    return lax.dynamic_index_in_dim(x, at, axis, keepdims=False)


def exchange(x, axis_name, step, size):
    return lax.ppermute(x, axis_name, [(j, j ^ step) for j in range(size)])


def over_cores(mine, give, n_occ, n_vir):
    held = mine + exchange(give, "vir", 1, n_vir)
    return held.reshape(held.shape[0], n_occ, n_vir // 2, held.shape[-1])


def over_plane(held, n_occ):
    occ = lax.axis_index("occ")
    total = pick(held, occ, 1)
    for s in range(1, n_occ):
        total = total + exchange(pick(held, occ ^ s, 1), "occ", s, n_occ)
    return total


def in_turn(held, index, axis_name, unit, size):
    step, count = 1, held.shape[1]
    while step < count:
        bit = (index // step) % 2
        parts = held.reshape(held.shape[0], -1, 2, *held.shape[2:])
        held = pick(parts, bit, 2) + exchange(pick(parts, 1 - bit, 2), axis_name, unit * step, size)
        step *= 2
    return held[:, 0]


def combine_kernel(me_ref, *refs, firsts):
    out_ref = refs[-1]
    n_z = len(refs) // 2
    plain = total = None
    for s in range(n_z):
        early = refs[s][...]
        value = jnp.concatenate([early[firsts:], refs[n_z + s][...]], axis=0)
        term = jnp.concatenate([value[m ^ 2 * s :][:1] for m in range(firsts)], axis=0) if s else value
        plain = plain + early[:firsts] if s else early[:firsts]
        total = total + term if s else term
    bit = 1
    while bit < firsts:
        other = jnp.concatenate([total[m ^ bit :][:1] for m in range(firsts)], axis=0)
        total = jnp.where((me_ref[0] & bit) != 0, other, total)
        bit *= 2
    out_ref[...] = jnp.concatenate([plain, total], axis=0).astype(out_ref.dtype)


def combined(early, late):
    columns = early[0].shape[1]
    firsts = (early[0].shape[0] + late[0].shape[0]) // 2
    block = columns // 2
    return pl.pallas_call(
        functools.partial(combine_kernel, firsts=firsts),
        grid_spec=pltpu.PrefetchScalarGridSpec(
            num_scalar_prefetch=1,
            grid=(columns // block,),
            in_specs=[pl.BlockSpec((x.shape[0], block), lambda n, at: (0, n)) for x in (*early, *late)],
            out_specs=pl.BlockSpec((2 * firsts, block), lambda n, at: (0, n)),
        ),
        out_shape=jax.ShapeDtypeStruct((2 * firsts, columns), jnp.bfloat16),
        name="combine",
    )(position(), *early, *late)


def along_z(sums, n_vir):
    z = lax.axis_index("vir") // 2
    return [pick(sums, z, 1)] + [exchange(pick(sums, z ^ s, 1), "vir", 2 * s, n_vir) for s in range(1, n_vir // 2)]


def on_block(amplitudes, integrals, screen, n_occ, n_vir):
    columns = integrals.shape[0] * integrals.shape[1]
    weights = integrals.reshape(columns, *integrals.shape[2:]).swapaxes(0, 1)
    n_z = n_vir // 2
    occ = lax.axis_index("occ")
    steps = list(range(n_z))
    soon, later = steps[:2], steps[2:]
    first = lax.all_to_all(screened(amplitudes, screen, n_occ, n_vir), "vir", 0, 0, tiled=True)

    give = given(amplitudes, screen, [(1, s) for s in steps], n_occ, n_vir, after=(weights,))
    got = exchange(give, "vir", 1, n_vir)
    last = []
    if soon:
        last += kept(amplitudes, screen, got, 1, 1, soon, 0, n_occ, n_vir)
    last += held_back(kept(amplitudes, screen, got, 1, 1, later, len(soon), n_occ, n_vir), (first,))
    last = [x if s == 0 else exchange(x, "vir", 2 * s, n_vir) for s, x in zip(steps, last)]

    def early(turn, _):
        held = over_cores(*product([first, *last[: len(soon)]], weights, 512, n_vir, turn), n_occ, n_vir)
        return in_turn(held, occ, "occ", 1, n_occ)

    once = 1 + lax.axis_index("vir") // n_vir
    units = n_vir + 2 * len(soon)
    early_sums = lax.fori_loop(0, once, early, jnp.zeros((units, n_z, columns), jnp.float32))
    mine, give = held_product(last[len(soon) :], held_in_vmem(weights, (early_sums,)), 512, True)
    early_terms = along_z(early_sums, n_vir)
    [give] = held_back([give], early_terms[:2])
    late_sums = over_plane(over_cores(mine, give, n_occ, n_vir), n_occ)
    return combined(early_terms, along_z(late_sums, n_vir))


def on_any(amplitudes, integrals, screen):
    keep_mask = jnp.repeat(screen, TILE, axis=2).astype(jnp.bfloat16)
    screened = amplitudes * keep_mask[None]
    columns = integrals.shape[0] * integrals.shape[1]
    flat_weights = integrals.reshape(columns, -1)
    relaid = lax.all_to_all(screened, "vir", split_axis=3, concat_axis=1, tiled=True)
    left_rows = relaid.reshape(-1, flat_weights.shape[1])
    partial_value = lax.dot_general(
        left_rows, flat_weights, (((1,), (1,)), ((), ())), preferred_element_type=jnp.float32
    )
    owned_rows = lax.psum_scatter(partial_value, ("occ", "vir"), scatter_dimension=0, tiled=True)
    return owned_rows.astype(jnp.bfloat16)


def solution(mesh):
    n_occ, n_vir = mesh.shape["occ"], mesh.shape["vir"]

    def on_device(amplitudes, integrals, screen):
        fits = n_occ == 4 and n_vir == 8
        if fits and amplitudes.shape[0] == 2 * n_occ * n_vir and amplitudes.shape[1] == 1:
            return on_block(amplitudes, integrals, screen, n_occ, n_vir)
        return on_any(amplitudes, integrals, screen)

    return jax.shard_map(
        on_device,
        mesh=mesh,
        in_specs=(P(None, "vir", "occ", None), P(None, None, "occ", "vir"), P("vir", "occ", None)),
        out_specs=P(("occ", "vir"), None),
        check_vma=False,
    )
```

```python
import functools

import jax
import jax.numpy as jnp
from jax import lax
from jax.experimental import pallas as pl
from jax.experimental.pallas import tpu as pltpu
from jax.sharding import PartitionSpec as P

TILE = 64
VMEM = 60 << 20
HELD = 12 << 20


def screen_block(amp, screen_ref, dest):
    depth, width = amp.shape[-2:]
    tiles = screen_ref.shape[-1]
    tile_at = lax.broadcasted_iota(jnp.int32, (tiles, width), 0)
    column = lax.broadcasted_iota(jnp.int32, (tiles, width), 1) + dest * width
    spread = (column // TILE == tile_at).astype(jnp.float32).astype(jnp.bfloat16)
    rows = screen_ref[0].astype(jnp.float32).astype(jnp.bfloat16)
    mask = jnp.dot(rows, spread, preferred_element_type=jnp.float32).astype(jnp.bfloat16)
    return jnp.swapaxes(amp.reshape(-1, depth, width) * mask[None], 0, 1)


def give_kernel(me_ref, amp_ref, screen_ref, *refs, steps):
    out_ref = refs[-1]
    step = steps[0]
    for at, other in enumerate(steps):
        step = jnp.where(pl.program_id(0) == at, other, step)
    out_ref[0] = screen_block(amp_ref[...], screen_ref, me_ref[0] ^ (2 * step + 1))


def keep_kernel(me_ref, *refs, steps, parts):
    screen_ref, given_refs = refs[len(steps)], refs[len(steps) + 1 : 2 * len(steps) + 1]
    out_refs = refs[len(refs) - len(steps) :]
    for at, step in enumerate(steps):
        out_refs[at][0] = screen_block(refs[at][...], screen_ref, me_ref[0] ^ (2 * step))
        out_refs[at][1] = given_refs[at][0]


def position():
    return lax.axis_index("vir").astype(jnp.int32).reshape(1)


def amplitude_view(amplitudes, n_occ, n_vir):
    return amplitudes.reshape(n_occ, n_vir // 2, 2, 2, *amplitudes.shape[2:])


def given(amplitudes, screen, units, n_occ, n_vir, after=()):
    depth, total = amplitudes.shape[2:]
    width, rows = total // n_vir, n_occ * n_vir // 2
    parts, steps = [u[0] for u in units], [u[1] for u in units]

    def choose(values, at):
        out = values[0]
        for n, value in enumerate(values):
            out = jnp.where(at == n, value, out)
        return out

    return pl.pallas_call(
        functools.partial(give_kernel, steps=steps),
        grid_spec=pltpu.PrefetchScalarGridSpec(
            num_scalar_prefetch=1,
            grid=(len(units), 2),
            in_specs=[
                pl.BlockSpec(
                    (n_occ, n_vir // 2, 1, 1, depth, width),
                    lambda u, c, at: (0, 0, c, choose(parts, u), 0, at[0] ^ (2 * choose(steps, u) + 1)),
                ),
                pl.BlockSpec(screen.shape, lambda u, c, at: (0, 0, 0)),
            ]
            + [pl.BlockSpec(memory_space=pl.ANY) for _ in after],
            out_specs=pl.BlockSpec((1, depth, rows, width), lambda u, c, at: (u, 0, c, 0)),
        ),
        out_shape=jax.ShapeDtypeStruct((len(units), depth, 2 * rows, width), jnp.bfloat16),
        compiler_params=pltpu.CompilerParams(vmem_limit_bytes=VMEM),
        cost_estimate=pl.CostEstimate(flops=0, bytes_accessed=0, transcendentals=0),
        name="give",
    )(position(), amplitude_view(amplitudes, n_occ, n_vir), screen, *after)


def kept(amplitudes, screen, got, first, parts, steps, base, n_occ, n_vir, after=()):
    depth, total = amplitudes.shape[2:]
    width, rows = total // n_vir, n_occ * n_vir // 2
    view = amplitude_view(amplitudes, n_occ, n_vir)

    def source(step):
        return pl.BlockSpec(
            (n_occ, n_vir // 2, 1, 1, depth, width), lambda p, c, at: (0, 0, c, first + p, 0, at[0] ^ (2 * step))
        )

    def sibling(n):
        return pl.BlockSpec((1, depth, rows, width), lambda p, c, at: (base + n * parts + p, 0, c, 0))

    return pl.pallas_call(
        functools.partial(keep_kernel, steps=steps, parts=parts),
        grid_spec=pltpu.PrefetchScalarGridSpec(
            num_scalar_prefetch=1,
            grid=(parts, 2),
            in_specs=[source(step) for step in steps]
            + [pl.BlockSpec(screen.shape, lambda p, c, at: (0, 0, 0))]
            + [sibling(n) for n in range(len(steps))]
            + [pl.BlockSpec(memory_space=pl.ANY) for _ in after],
            out_specs=[pl.BlockSpec((2, depth, rows, width), lambda p, c, at: (p, 0, c, 0)) for _ in steps],
        ),
        out_shape=[jax.ShapeDtypeStruct((2 * parts, depth, 2 * rows, width), jnp.bfloat16) for _ in steps],
        compiler_params=pltpu.CompilerParams(vmem_limit_bytes=VMEM),
        cost_estimate=pl.CostEstimate(flops=0, bytes_accessed=0, transcendentals=0),
        name="keep",
    )(position(), *[view] * len(steps), screen, *[got] * len(steps), *after)


def screen_kernel(*refs, dests):
    screen_ref, out_ref = refs[-2:]
    width = out_ref.shape[-1]
    per = screen_ref.shape[-1] // dests
    tile_at = lax.broadcasted_iota(jnp.int32, (per, width), 0)
    column = lax.broadcasted_iota(jnp.int32, (per, width), 1)
    spread = (column // TILE == tile_at).astype(jnp.float32).astype(jnp.bfloat16)
    rows = screen_ref[0].astype(jnp.float32).astype(jnp.bfloat16)
    for dest in range(dests):
        mask = jnp.dot(rows[:, dest * per : (dest + 1) * per], spread, preferred_element_type=jnp.float32)
        mask = mask.astype(jnp.bfloat16)[None]
        for core in range(2):
            block = refs[dest][:, :, core, 0]
            block = block.reshape(-1, *block.shape[2:])
            count = block.shape[0]
            out_ref[dest, :, core * count : (core + 1) * count] = jnp.swapaxes(block * mask, 0, 1)


def screened(amplitudes, screen, n_occ, n_vir):
    depth, total = amplitudes.shape[2:]
    width, n_z = total // n_vir, n_vir // 2
    some, rows = depth // 2, n_occ * n_vir

    def source(dest):
        return pl.BlockSpec((n_occ, n_z, 2, 1, some, width), lambda k: (0, 0, 0, 0, k, dest))

    return pl.pallas_call(
        functools.partial(screen_kernel, dests=n_vir),
        grid=(2,),
        in_specs=[source(dest) for dest in range(n_vir)]
        + [pl.BlockSpec((1, some, screen.shape[2]), lambda k: (0, k, 0))],
        out_specs=pl.BlockSpec((n_vir, some, rows, width), lambda k: (0, k, 0, 0)),
        out_shape=jax.ShapeDtypeStruct((n_vir, depth, rows, width), jnp.bfloat16),
        compiler_params=pltpu.CompilerParams(vmem_limit_bytes=VMEM),
        cost_estimate=pl.CostEstimate(flops=0, bytes_accessed=0, transcendentals=0),
        name="screen",
    )(*[amplitude_view(amplitudes, n_occ, n_vir)] * n_vir, screen)


def gate_kernel(*refs):
    del refs


def held_back(arrays, after):
    return pl.pallas_call(
        gate_kernel,
        in_specs=[pl.BlockSpec(memory_space=pl.ANY)] * (len(arrays) + len(after)),
        out_specs=[pl.BlockSpec(memory_space=pl.ANY)] * len(arrays),
        out_shape=[jax.ShapeDtypeStruct(x.shape, x.dtype) for x in arrays],
        input_output_aliases={n: n for n in range(len(arrays))},
        cost_estimate=pl.CostEstimate(flops=0, bytes_accessed=0, transcendentals=0),
        name="gate",
    )(*arrays, *after)


def product_kernel(me_ref, *refs, count, plain):
    left_refs, weight_ref, mine_ref, give_ref = refs[:count], refs[count], refs[-2], refs[-1]
    piece = mine_ref.shape[1]
    total = None
    for k in range(weight_ref.shape[0]):
        left = [ref[unit, k] for ref in left_refs for unit in range(ref.shape[0])]
        term = lax.dot_general(
            jnp.concatenate(left, axis=0),
            weight_ref[k],
            (((1,), (1,)), ((), ())),
            preferred_element_type=jnp.float32,
        )
        total = term if total is None else total + term
    odd = me_ref[0] % 2 == 1
    for unit in range(mine_ref.shape[0]):
        zero, one = (total[(2 * unit + core) * piece : (2 * unit + core + 1) * piece] for core in range(2))
        mine_ref[unit] = jnp.where(odd, one, zero)
        give_ref[unit if unit < plain else unit ^ 1] = jnp.where(odd, zero, one)


def product(lefts, weights, block, plain, turn=0, after=()):
    columns = weights.shape[1]
    shape = (sum(x.shape[0] for x in lefts), lefts[0].shape[2] // 2, columns)
    out_spec = pl.BlockSpec((*shape[:-1], block), lambda n, at: (0, 0, n))
    return pl.pallas_call(
        functools.partial(product_kernel, count=len(lefts), plain=plain),
        grid_spec=pltpu.PrefetchScalarGridSpec(
            num_scalar_prefetch=1,
            grid=(columns // block,),
            in_specs=[pl.BlockSpec(x.shape, lambda n, at: (0, 0, 0, 0)) for x in lefts]
            + [pl.BlockSpec((weights.shape[0], block, weights.shape[2]), lambda n, at: (0, n, 0))]
            + [pl.BlockSpec(memory_space=pl.ANY) for _ in after],
            out_specs=[out_spec, out_spec],
        ),
        out_shape=[jax.ShapeDtypeStruct(shape, jnp.float32)] * 2,
        compiler_params=pltpu.CompilerParams(vmem_limit_bytes=VMEM),
        cost_estimate=pl.CostEstimate(flops=0, bytes_accessed=0, transcendentals=0),
        name="product",
    )(position() + 2 * turn, *lefts, weights, *after)


def hold_kernel(weight_ref, *refs):
    out_ref, sems = refs[-2:]
    copies = [
        pltpu.make_async_copy(weight_ref.at[k], out_ref.at[k], sems.at[k]) for k in range(weight_ref.shape[0])
    ]
    for copy in copies:
        copy.start()
    for copy in copies:
        copy.wait()


def held_in_vmem(weights, after):
    return pl.pallas_call(
        hold_kernel,
        in_specs=[pl.BlockSpec(memory_space=pl.ANY)] * (1 + len(after)),
        out_specs=pl.BlockSpec(memory_space=pltpu.VMEM),
        out_shape=pltpu.VMEM(weights.shape, weights.dtype),
        scratch_shapes=[pltpu.SemaphoreType.DMA((weights.shape[0],))],
        compiler_params=pltpu.CompilerParams(vmem_limit_bytes=1 << 20),
        cost_estimate=pl.CostEstimate(flops=0, bytes_accessed=0, transcendentals=0),
        name="hold",
    )(weights, *after)


def held_product_kernel(*refs, count, block, turned):
    left_refs, weight_ref, (mine_ref, give_ref) = refs[:count], refs[count], refs[-2:]
    piece, columns = mine_ref.shape[1:]
    odd = lax.axis_index("vir") % 2 == 1

    @pl.loop(0, columns // block)
    def _(n):
        at = pl.multiple_of(n * block, block)
        total = None
        for k in range(weight_ref.shape[0]):
            left = jnp.concatenate([ref[unit, k] for ref in left_refs for unit in range(ref.shape[0])], axis=0)
            weight = weight_ref[k, pl.ds(at, block)]
            term = lax.dot_general(
                *((weight, left) if turned else (left, weight)),
                (((1,), (1,)), ((), ())),
                preferred_element_type=jnp.float32,
            )
            total = term if total is None else total + term
        if turned:
            total = total.T
        for unit in range(mine_ref.shape[0]):
            zero, one = (total[(2 * unit + core) * piece : (2 * unit + core + 1) * piece] for core in range(2))
            mine_ref[unit, :, pl.ds(at, block)] = jnp.where(odd, one, zero)
            give_ref[unit ^ 1, :, pl.ds(at, block)] = jnp.where(odd, zero, one)


def held_product(lefts, weights, block, turned, after=()):
    shape = (sum(x.shape[0] for x in lefts), lefts[0].shape[2] // 2, weights.shape[1])
    return pl.pallas_call(
        functools.partial(held_product_kernel, count=len(lefts), block=block, turned=turned),
        in_specs=[pl.BlockSpec(memory_space=pltpu.VMEM)] * (1 + len(lefts))
        + [pl.BlockSpec(memory_space=pl.ANY)] * len(after),
        out_specs=[pl.BlockSpec(memory_space=pltpu.VMEM)] * 2,
        out_shape=[jax.ShapeDtypeStruct(shape, jnp.float32)] * 2,
        compiler_params=pltpu.CompilerParams(vmem_limit_bytes=HELD),
        cost_estimate=pl.CostEstimate(flops=0, bytes_accessed=0, transcendentals=0),
        name="product_held",
    )(*lefts, weights, *after)


def pick(x, at, axis):
    return lax.dynamic_index_in_dim(x, at, axis, keepdims=False)


def exchange(x, axis_name, step, size):
    return lax.ppermute(x, axis_name, [(j, j ^ step) for j in range(size)])


def over_cores(mine, give, n_occ, n_vir):
    held = mine + exchange(give, "vir", 1, n_vir)
    return held.reshape(held.shape[0], n_occ, n_vir // 2, held.shape[-1])


def over_plane(held, n_occ):
    occ = lax.axis_index("occ")
    total = pick(held, occ, 1)
    for s in range(1, n_occ):
        total = total + exchange(pick(held, occ ^ s, 1), "occ", s, n_occ)
    return total


def in_turn(held, index, axis_name, unit, size):
    step, count = 1, held.shape[1]
    while step < count:
        bit = (index // step) % 2
        parts = held.reshape(held.shape[0], -1, 2, *held.shape[2:])
        held = pick(parts, bit, 2) + exchange(pick(parts, 1 - bit, 2), axis_name, unit * step, size)
        step *= 2
    return held[:, 0]


def combine_kernel(me_ref, *refs, firsts):
    out_ref = refs[-1]
    n_z = len(refs) // 2
    plain = total = None
    for s in range(n_z):
        early = refs[s][...]
        value = jnp.concatenate([early[firsts:], refs[n_z + s][...]], axis=0)
        term = jnp.concatenate([value[m ^ 2 * s :][:1] for m in range(firsts)], axis=0) if s else value
        plain = plain + early[:firsts] if s else early[:firsts]
        total = total + term if s else term
    bit = 1
    while bit < firsts:
        other = jnp.concatenate([total[m ^ bit :][:1] for m in range(firsts)], axis=0)
        total = jnp.where((me_ref[0] & bit) != 0, other, total)
        bit *= 2
    out_ref[...] = jnp.concatenate([plain, total], axis=0).astype(out_ref.dtype)


def combined(early, late):
    columns = early[0].shape[1]
    firsts = (early[0].shape[0] + late[0].shape[0]) // 2
    vmem = pl.BlockSpec(memory_space=pltpu.VMEM)
    return pl.pallas_call(
        functools.partial(combine_kernel, firsts=firsts),
        in_specs=[pl.BlockSpec(memory_space=pltpu.SMEM)] + [vmem] * (len(early) + len(late)),
        out_specs=vmem,
        out_shape=jax.ShapeDtypeStruct((2 * firsts, columns), jnp.bfloat16),
        compiler_params=pltpu.CompilerParams(vmem_limit_bytes=8 << 20),
        name="combine",
    )(position(), *early, *late)


def along_z(sums, n_vir):
    z = lax.axis_index("vir") // 2
    return [pick(sums, z, 1)] + [exchange(pick(sums, z ^ s, 1), "vir", 2 * s, n_vir) for s in range(1, n_vir // 2)]


def on_block(amplitudes, integrals, screen, n_occ, n_vir):
    columns = integrals.shape[0] * integrals.shape[1]
    weights = integrals.reshape(columns, *integrals.shape[2:]).swapaxes(0, 1)
    n_z = n_vir // 2
    occ = lax.axis_index("occ")
    steps = list(range(n_z))
    soon, later = steps[:2], steps[2:]
    first = lax.all_to_all(screened(amplitudes, screen, n_occ, n_vir), "vir", 0, 0, tiled=True)

    give = given(amplitudes, screen, [(1, s) for s in steps], n_occ, n_vir, after=(weights,))
    got = exchange(give, "vir", 1, n_vir)
    last = []
    if soon:
        last += kept(amplitudes, screen, got, 1, 1, soon, 0, n_occ, n_vir)
    last += held_back(kept(amplitudes, screen, got, 1, 1, later, len(soon), n_occ, n_vir), (first,))
    last = [x if s == 0 else exchange(x, "vir", 2 * s, n_vir) for s, x in zip(steps, last)]

    def early(turn, _):
        held = over_cores(*product([first, *last[: len(soon)]], weights, 512, n_vir, turn), n_occ, n_vir)
        return in_turn(held, occ, "occ", 1, n_occ)

    once = 1 + lax.axis_index("vir") // n_vir
    units = n_vir + 2 * len(soon)
    early_sums = lax.fori_loop(0, once, early, jnp.zeros((units, n_z, columns), jnp.float32))
    early_terms = along_z(early_sums, n_vir)
    held = held_in_vmem(weights, (early_sums,))
    mine, give = held_product(last[len(soon) :], held, 512, True, after=early_terms[1:2])
    late_sums = over_plane(over_cores(mine, give, n_occ, n_vir), n_occ)
    return combined(early_terms, along_z(late_sums, n_vir))


def on_any(amplitudes, integrals, screen):
    keep_mask = jnp.repeat(screen, TILE, axis=2).astype(jnp.bfloat16)
    screened = amplitudes * keep_mask[None]
    columns = integrals.shape[0] * integrals.shape[1]
    flat_weights = integrals.reshape(columns, -1)
    relaid = lax.all_to_all(screened, "vir", split_axis=3, concat_axis=1, tiled=True)
    left_rows = relaid.reshape(-1, flat_weights.shape[1])
    partial_value = lax.dot_general(
        left_rows, flat_weights, (((1,), (1,)), ((), ())), preferred_element_type=jnp.float32
    )
    owned_rows = lax.psum_scatter(partial_value, ("occ", "vir"), scatter_dimension=0, tiled=True)
    return owned_rows.astype(jnp.bfloat16)


def solution(mesh):
    n_occ, n_vir = mesh.shape["occ"], mesh.shape["vir"]

    def on_device(amplitudes, integrals, screen):
        fits = n_occ == 4 and n_vir == 8
        if fits and amplitudes.shape[0] == 2 * n_occ * n_vir and amplitudes.shape[1] == 1:
            return on_block(amplitudes, integrals, screen, n_occ, n_vir)
        return on_any(amplitudes, integrals, screen)

    return jax.shard_map(
        on_device,
        mesh=mesh,
        in_specs=(P(None, "vir", "occ", None), P(None, None, "occ", "vir"), P("vir", "occ", None)),
        out_specs=P(("occ", "vir"), None),
        check_vma=False,
    )
```

```python
import functools

import jax
import jax.numpy as jnp
from jax import lax
from jax.experimental import pallas as pl
from jax.experimental.pallas import tpu as pltpu
from jax.sharding import PartitionSpec as P

TILE = 64
VMEM = 60 << 20
HELD = 12 << 20


def screen_block(amp, screen_ref, dest):
    depth, width = amp.shape[-2:]
    tiles = screen_ref.shape[-1]
    tile_at = lax.broadcasted_iota(jnp.int32, (tiles, width), 0)
    column = lax.broadcasted_iota(jnp.int32, (tiles, width), 1) + dest * width
    spread = (column // TILE == tile_at).astype(jnp.float32).astype(jnp.bfloat16)
    rows = screen_ref[0].astype(jnp.float32).astype(jnp.bfloat16)
    mask = jnp.dot(rows, spread, preferred_element_type=jnp.float32).astype(jnp.bfloat16)
    return jnp.swapaxes(amp.reshape(-1, depth, width) * mask[None], 0, 1)


def give_kernel(me_ref, amp_ref, screen_ref, *refs, steps):
    out_ref = refs[-1]
    step = steps[0]
    for at, other in enumerate(steps):
        step = jnp.where(pl.program_id(0) == at, other, step)
    out_ref[0] = screen_block(amp_ref[...], screen_ref, me_ref[0] ^ (2 * step + 1))


def keep_kernel(me_ref, *refs, steps, parts):
    screen_ref, given_refs = refs[len(steps)], refs[len(steps) + 1 : 2 * len(steps) + 1]
    out_refs = refs[len(refs) - len(steps) :]
    for at, step in enumerate(steps):
        out_refs[at][0] = screen_block(refs[at][...], screen_ref, me_ref[0] ^ (2 * step))
        out_refs[at][1] = given_refs[at][0]


def position():
    return lax.axis_index("vir").astype(jnp.int32).reshape(1)


def amplitude_view(amplitudes, n_occ, n_vir):
    return amplitudes.reshape(n_occ, n_vir // 2, 2, 2, *amplitudes.shape[2:])


def given(amplitudes, screen, units, n_occ, n_vir, after=()):
    depth, total = amplitudes.shape[2:]
    width, rows = total // n_vir, n_occ * n_vir // 2
    parts, steps = [u[0] for u in units], [u[1] for u in units]

    def choose(values, at):
        out = values[0]
        for n, value in enumerate(values):
            out = jnp.where(at == n, value, out)
        return out

    return pl.pallas_call(
        functools.partial(give_kernel, steps=steps),
        grid_spec=pltpu.PrefetchScalarGridSpec(
            num_scalar_prefetch=1,
            grid=(len(units), 2),
            in_specs=[
                pl.BlockSpec(
                    (n_occ, n_vir // 2, 1, 1, depth, width),
                    lambda u, c, at: (0, 0, c, choose(parts, u), 0, at[0] ^ (2 * choose(steps, u) + 1)),
                ),
                pl.BlockSpec(screen.shape, lambda u, c, at: (0, 0, 0)),
            ]
            + [pl.BlockSpec(memory_space=pl.ANY) for _ in after],
            out_specs=pl.BlockSpec((1, depth, rows, width), lambda u, c, at: (u, 0, c, 0)),
        ),
        out_shape=jax.ShapeDtypeStruct((len(units), depth, 2 * rows, width), jnp.bfloat16),
        compiler_params=pltpu.CompilerParams(vmem_limit_bytes=VMEM),
        cost_estimate=pl.CostEstimate(flops=0, bytes_accessed=0, transcendentals=0),
        name="give",
    )(position(), amplitude_view(amplitudes, n_occ, n_vir), screen, *after)


def kept(amplitudes, screen, got, first, parts, steps, base, n_occ, n_vir, after=()):
    depth, total = amplitudes.shape[2:]
    width, rows = total // n_vir, n_occ * n_vir // 2
    view = amplitude_view(amplitudes, n_occ, n_vir)

    def source(step):
        return pl.BlockSpec(
            (n_occ, n_vir // 2, 1, 1, depth, width), lambda p, c, at: (0, 0, c, first + p, 0, at[0] ^ (2 * step))
        )

    def sibling(n):
        return pl.BlockSpec((1, depth, rows, width), lambda p, c, at: (base + n * parts + p, 0, c, 0))

    return pl.pallas_call(
        functools.partial(keep_kernel, steps=steps, parts=parts),
        grid_spec=pltpu.PrefetchScalarGridSpec(
            num_scalar_prefetch=1,
            grid=(parts, 2),
            in_specs=[source(step) for step in steps]
            + [pl.BlockSpec(screen.shape, lambda p, c, at: (0, 0, 0))]
            + [sibling(n) for n in range(len(steps))]
            + [pl.BlockSpec(memory_space=pl.ANY) for _ in after],
            out_specs=[pl.BlockSpec((2, depth, rows, width), lambda p, c, at: (p, 0, c, 0)) for _ in steps],
        ),
        out_shape=[jax.ShapeDtypeStruct((2 * parts, depth, 2 * rows, width), jnp.bfloat16) for _ in steps],
        compiler_params=pltpu.CompilerParams(vmem_limit_bytes=VMEM),
        cost_estimate=pl.CostEstimate(flops=0, bytes_accessed=0, transcendentals=0),
        name="keep",
    )(position(), *[view] * len(steps), screen, *[got] * len(steps), *after)


def screen_kernel(*refs, dests):
    screen_ref, out_ref = refs[-2:]
    width = out_ref.shape[-1]
    per = screen_ref.shape[-1] // dests
    tile_at = lax.broadcasted_iota(jnp.int32, (per, width), 0)
    column = lax.broadcasted_iota(jnp.int32, (per, width), 1)
    spread = (column // TILE == tile_at).astype(jnp.float32).astype(jnp.bfloat16)
    rows = screen_ref[0].astype(jnp.float32).astype(jnp.bfloat16)
    for dest in range(dests):
        mask = jnp.dot(rows[:, dest * per : (dest + 1) * per], spread, preferred_element_type=jnp.float32)
        mask = mask.astype(jnp.bfloat16)[None]
        for core in range(2):
            block = refs[dest][:, :, core, 0]
            block = block.reshape(-1, *block.shape[2:])
            count = block.shape[0]
            out_ref[dest, :, core * count : (core + 1) * count] = jnp.swapaxes(block * mask, 0, 1)


def screened(amplitudes, screen, n_occ, n_vir):
    depth, total = amplitudes.shape[2:]
    width, n_z = total // n_vir, n_vir // 2
    some, rows = depth // 2, n_occ * n_vir

    def source(dest):
        return pl.BlockSpec((n_occ, n_z, 2, 1, some, width), lambda k: (0, 0, 0, 0, k, dest))

    return pl.pallas_call(
        functools.partial(screen_kernel, dests=n_vir),
        grid=(2,),
        in_specs=[source(dest) for dest in range(n_vir)]
        + [pl.BlockSpec((1, some, screen.shape[2]), lambda k: (0, k, 0))],
        out_specs=pl.BlockSpec((n_vir, some, rows, width), lambda k: (0, k, 0, 0)),
        out_shape=jax.ShapeDtypeStruct((n_vir, depth, rows, width), jnp.bfloat16),
        compiler_params=pltpu.CompilerParams(vmem_limit_bytes=VMEM),
        cost_estimate=pl.CostEstimate(flops=0, bytes_accessed=0, transcendentals=0),
        name="screen",
    )(*[amplitude_view(amplitudes, n_occ, n_vir)] * n_vir, screen)


def gate_kernel(*refs):
    del refs


def held_back(arrays, after):
    return pl.pallas_call(
        gate_kernel,
        in_specs=[pl.BlockSpec(memory_space=pl.ANY)] * (len(arrays) + len(after)),
        out_specs=[pl.BlockSpec(memory_space=pl.ANY)] * len(arrays),
        out_shape=[jax.ShapeDtypeStruct(x.shape, x.dtype) for x in arrays],
        input_output_aliases={n: n for n in range(len(arrays))},
        cost_estimate=pl.CostEstimate(flops=0, bytes_accessed=0, transcendentals=0),
        name="gate",
    )(*arrays, *after)


def product_kernel(me_ref, *refs, count, plain):
    left_refs, weight_ref, mine_ref, give_ref = refs[:count], refs[count], refs[-2], refs[-1]
    piece = mine_ref.shape[1]
    total = None
    for k in range(weight_ref.shape[0]):
        left = [ref[unit, k] for ref in left_refs for unit in range(ref.shape[0])]
        term = lax.dot_general(
            jnp.concatenate(left, axis=0),
            weight_ref[k],
            (((1,), (1,)), ((), ())),
            preferred_element_type=jnp.float32,
        )
        total = term if total is None else total + term
    odd = me_ref[0] % 2 == 1
    for unit in range(mine_ref.shape[0]):
        zero, one = (total[(2 * unit + core) * piece : (2 * unit + core + 1) * piece] for core in range(2))
        mine_ref[unit] = jnp.where(odd, one, zero)
        give_ref[unit if unit < plain else unit ^ 1] = jnp.where(odd, zero, one)


def product(lefts, weights, block, plain, turn=0, after=()):
    columns = weights.shape[1]
    shape = (sum(x.shape[0] for x in lefts), lefts[0].shape[2] // 2, columns)
    out_spec = pl.BlockSpec((*shape[:-1], block), lambda n, at: (0, 0, n))
    return pl.pallas_call(
        functools.partial(product_kernel, count=len(lefts), plain=plain),
        grid_spec=pltpu.PrefetchScalarGridSpec(
            num_scalar_prefetch=1,
            grid=(columns // block,),
            in_specs=[pl.BlockSpec(x.shape, lambda n, at: (0, 0, 0, 0)) for x in lefts]
            + [pl.BlockSpec((weights.shape[0], block, weights.shape[2]), lambda n, at: (0, n, 0))]
            + [pl.BlockSpec(memory_space=pl.ANY) for _ in after],
            out_specs=[out_spec, out_spec],
        ),
        out_shape=[jax.ShapeDtypeStruct(shape, jnp.float32)] * 2,
        compiler_params=pltpu.CompilerParams(vmem_limit_bytes=VMEM),
        cost_estimate=pl.CostEstimate(flops=0, bytes_accessed=0, transcendentals=0),
        name="product",
    )(position() + 2 * turn, *lefts, weights, *after)


def hold_kernel(weight_ref, *refs):
    out_ref, sems = refs[-2:]
    copies = [
        pltpu.make_async_copy(weight_ref.at[k], out_ref.at[k], sems.at[k]) for k in range(weight_ref.shape[0])
    ]
    for copy in copies:
        copy.start()
    for copy in copies:
        copy.wait()


def held_in_vmem(weights, after):
    return pl.pallas_call(
        hold_kernel,
        in_specs=[pl.BlockSpec(memory_space=pl.ANY)] * (1 + len(after)),
        out_specs=pl.BlockSpec(memory_space=pltpu.VMEM),
        out_shape=pltpu.VMEM(weights.shape, weights.dtype),
        scratch_shapes=[pltpu.SemaphoreType.DMA((weights.shape[0],))],
        compiler_params=pltpu.CompilerParams(vmem_limit_bytes=1 << 20),
        cost_estimate=pl.CostEstimate(flops=0, bytes_accessed=0, transcendentals=0),
        name="hold",
    )(weights, *after)


def held_product_kernel(*refs, count, block, turned):
    left_refs, weight_ref, (mine_ref, give_ref) = refs[:count], refs[count], refs[-2:]
    piece, columns = mine_ref.shape[1:]
    odd = lax.axis_index("vir") % 2 == 1

    @pl.loop(0, columns // block)
    def _(n):
        at = pl.multiple_of(n * block, block)
        total = None
        for k in range(weight_ref.shape[0]):
            left = jnp.concatenate([ref[unit, k] for ref in left_refs for unit in range(ref.shape[0])], axis=0)
            weight = weight_ref[k, pl.ds(at, block)]
            term = lax.dot_general(
                *((weight, left) if turned else (left, weight)),
                (((1,), (1,)), ((), ())),
                preferred_element_type=jnp.float32,
            )
            total = term if total is None else total + term
        if turned:
            total = total.T
        for unit in range(mine_ref.shape[0]):
            zero, one = (total[(2 * unit + core) * piece : (2 * unit + core + 1) * piece] for core in range(2))
            mine_ref[unit, :, pl.ds(at, block)] = jnp.where(odd, one, zero)
            give_ref[unit ^ 1, :, pl.ds(at, block)] = jnp.where(odd, zero, one)


def held_product(lefts, weights, block, turned, after=()):
    shape = (sum(x.shape[0] for x in lefts), lefts[0].shape[2] // 2, weights.shape[1])
    return pl.pallas_call(
        functools.partial(held_product_kernel, count=len(lefts), block=block, turned=turned),
        in_specs=[pl.BlockSpec(memory_space=pltpu.VMEM)] * (1 + len(lefts))
        + [pl.BlockSpec(memory_space=pl.ANY)] * len(after),
        out_specs=[pl.BlockSpec(memory_space=pltpu.VMEM)] * 2,
        out_shape=[jax.ShapeDtypeStruct(shape, jnp.float32)] * 2,
        compiler_params=pltpu.CompilerParams(vmem_limit_bytes=HELD),
        cost_estimate=pl.CostEstimate(flops=0, bytes_accessed=0, transcendentals=0),
        name="product_held",
    )(*lefts, weights, *after)


def pick(x, at, axis):
    return lax.dynamic_index_in_dim(x, at, axis, keepdims=False)


def exchange(x, axis_name, step, size):
    return lax.ppermute(x, axis_name, [(j, j ^ step) for j in range(size)])


def over_cores(mine, give, n_occ, n_vir):
    held = mine + exchange(give, "vir", 1, n_vir)
    return held.reshape(held.shape[0], n_occ, n_vir // 2, held.shape[-1])


def over_plane(held, n_occ):
    occ = lax.axis_index("occ")
    total = pick(held, occ, 1)
    for s in range(1, n_occ):
        total = total + exchange(pick(held, occ ^ s, 1), "occ", s, n_occ)
    return total


def in_turn(held, index, axis_name, unit, size):
    step, count = 1, held.shape[1]
    while step < count:
        bit = (index // step) % 2
        parts = held.reshape(held.shape[0], -1, 2, *held.shape[2:])
        held = pick(parts, bit, 2) + exchange(pick(parts, 1 - bit, 2), axis_name, unit * step, size)
        step *= 2
    return held[:, 0]


def combine_kernel(me_ref, *refs, firsts):
    out_ref = refs[-1]
    n_z = len(refs) // 2
    plain = total = None
    for s in range(n_z):
        early = refs[s][...]
        value = jnp.concatenate([early[firsts:], refs[n_z + s][...]], axis=0)
        term = jnp.concatenate([value[m ^ 2 * s :][:1] for m in range(firsts)], axis=0) if s else value
        plain = plain + early[:firsts] if s else early[:firsts]
        total = total + term if s else term
    bit = 1
    while bit < firsts:
        other = jnp.concatenate([total[m ^ bit :][:1] for m in range(firsts)], axis=0)
        total = jnp.where((me_ref[0] & bit) != 0, other, total)
        bit *= 2
    out_ref[...] = jnp.concatenate([plain, total], axis=0).astype(out_ref.dtype)


def combined(early, late):
    columns = early[0].shape[1]
    firsts = (early[0].shape[0] + late[0].shape[0]) // 2
    vmem = pl.BlockSpec(memory_space=pltpu.VMEM)
    return pl.pallas_call(
        functools.partial(combine_kernel, firsts=firsts),
        in_specs=[pl.BlockSpec(memory_space=pltpu.SMEM)] + [vmem] * (len(early) + len(late)),
        out_specs=vmem,
        out_shape=jax.ShapeDtypeStruct((2 * firsts, columns), jnp.bfloat16),
        compiler_params=pltpu.CompilerParams(vmem_limit_bytes=8 << 20),
        name="combine",
    )(position(), *early, *late)


def along_z(sums, n_vir):
    z = lax.axis_index("vir") // 2
    return [pick(sums, z, 1)] + [exchange(pick(sums, z ^ s, 1), "vir", 2 * s, n_vir) for s in range(1, n_vir // 2)]


def on_block(amplitudes, integrals, screen, n_occ, n_vir):
    columns = integrals.shape[0] * integrals.shape[1]
    weights = integrals.reshape(columns, *integrals.shape[2:]).swapaxes(0, 1)
    n_z = n_vir // 2
    occ = lax.axis_index("occ")
    steps = list(range(n_z))
    soon, later = steps[:2], steps[2:]
    first = lax.all_to_all(screened(amplitudes, screen, n_occ, n_vir), "vir", 0, 0, tiled=True)

    give = given(amplitudes, screen, [(1, s) for s in steps], n_occ, n_vir, after=(weights,))
    got = exchange(give, "vir", 1, n_vir)
    last = []
    if soon:
        last += kept(amplitudes, screen, got, 1, 1, soon, 0, n_occ, n_vir)
    last += held_back(kept(amplitudes, screen, got, 1, 1, later, len(soon), n_occ, n_vir), (first,))
    last = [x if s == 0 else exchange(x, "vir", 2 * s, n_vir) for s, x in zip(steps, last)]

    def early(turn, _):
        held = over_cores(*product([first, *last[: len(soon)]], weights, 512, n_vir, turn), n_occ, n_vir)
        return in_turn(held, occ, "occ", 1, n_occ)

    once = 1 + lax.axis_index("vir") // n_vir
    units = n_vir + 2 * len(soon)
    early_sums = lax.fori_loop(0, once, early, jnp.zeros((units, n_z, columns), jnp.float32))
    early_terms = along_z(early_sums, n_vir)
    held = held_in_vmem(weights, (early_sums,))
    mine, give = held_product(last[len(soon) :], held, 1024, True, after=early_terms[1:2])
    late_sums = over_plane(over_cores(mine, give, n_occ, n_vir), n_occ)
    return combined(early_terms, along_z(late_sums, n_vir))


def on_any(amplitudes, integrals, screen):
    keep_mask = jnp.repeat(screen, TILE, axis=2).astype(jnp.bfloat16)
    screened = amplitudes * keep_mask[None]
    columns = integrals.shape[0] * integrals.shape[1]
    flat_weights = integrals.reshape(columns, -1)
    relaid = lax.all_to_all(screened, "vir", split_axis=3, concat_axis=1, tiled=True)
    left_rows = relaid.reshape(-1, flat_weights.shape[1])
    partial_value = lax.dot_general(
        left_rows, flat_weights, (((1,), (1,)), ((), ())), preferred_element_type=jnp.float32
    )
    owned_rows = lax.psum_scatter(partial_value, ("occ", "vir"), scatter_dimension=0, tiled=True)
    return owned_rows.astype(jnp.bfloat16)


def solution(mesh):
    n_occ, n_vir = mesh.shape["occ"], mesh.shape["vir"]

    def on_device(amplitudes, integrals, screen):
        fits = n_occ == 4 and n_vir == 8
        if fits and amplitudes.shape[0] == 2 * n_occ * n_vir and amplitudes.shape[1] == 1:
            return on_block(amplitudes, integrals, screen, n_occ, n_vir)
        return on_any(amplitudes, integrals, screen)

    return jax.shard_map(
        on_device,
        mesh=mesh,
        in_specs=(P(None, "vir", "occ", None), P(None, None, "occ", "vir"), P("vir", "occ", None)),
        out_specs=P(("occ", "vir"), None),
        check_vma=False,
    )
```
